32 devices in a mesh: gz: 8 (over z, x), gx: 4 (over y, core).
Axes of the slice: x: 2, y: 2, z: 4, core: 2. Of those that a mesh axis runs over, the one named last changes fastest.
Arguments:
- d_field: float32 [3, 64, 128, 128], P(None, 'gz', 'gx'), may hold values from -6 to 6
- e_field: float32 [3, 64, 128, 128], P(None, 'gz', 'gx'), may hold values from -6 to 6
- h_field: float32 [3, 64, 128, 128], P(None, 'gz', 'gx'), may hold values from -6 to 6
- permittivity: float32 [64, 128, 128], P('gz', 'gx'), may hold values from 1 to 4
- kerr_coeff: float32 [64, 128, 128], P('gz', 'gx'), may hold values from 0.05 to 0.3
- classes: int32 [2, 128, 128], P(None, 'gx'), may hold values from 0 to 7
- eps_table: float32 [8], replicated, may hold values from 1 to 6
- chi_table: float32 [8], replicated, may hold values from 0.02 to 0.4
Outputs:
- d_out: float32 [3, 64, 128, 128], P(None, 'gz', 'gx')
- e_out: float32 [3, 64, 128, 128], P(None, 'gz', 'gx')
- h_out: float32 [3, 64, 128, 128], P(None, 'gz', 'gx')
- eps_out: float32 [64, 128, 128], P('gz', 'gx')
- chi_out: float32 [64, 128, 128], P('gz', 'gx')
The draws below stay inside these ranges and needn't reach their ends.
All inputs are finite; a program needn't handle non-finite values.
Results may differ from the reference program's by a relative error of at most 0.00002.
Values sent between devices are 32-bit elements; how exact they have to be, the bound alone decides.
A program may use at most 64 MiB of HBM per device.

```python
import math
import jax
import jax.numpy as jnp
from jax import lax

NX = 128
NY = 128
STEPS = 4
KERR = 3
ADVANCE = 2
CLASSES = 8
NZ = 64


def plant(result, key, smallest, top_value):
    extent = result.shape
    index_at = [jax.random.randint(jax.random.fold_in(key, axis), (), 0, extent[axis]) for axis in range(len(extent))]
    result = result.at[tuple(index_at)].set(smallest)
    longest = extent.index(max(extent))
    index_at[longest] = (index_at[longest] + 1) % extent[longest]
    return result.at[tuple(index_at)].set(top_value)


def block_levels(own_key, shape, pieces, smallest, top_value):
    loudness = 1.0
    for position, shards_of in pieces:
        steps = jax.random.uniform(jax.random.fold_in(jax.random.fold_in(own_key, 6), position), (shards_of,), jnp.float32, smallest / len(pieces), top_value / len(pieces))
        loudness = loudness * jnp.repeat(jnp.exp(steps), shape[position] // shards_of).reshape((-1,) + (1,) * (len(shape) - 1 - position))
    return loudness


def normal_values(stream_key, extent, scale, most, cuts=(), held_as=jnp.bfloat16):
    factor_of = block_levels(stream_key, extent, cuts, -0.22, 0.18) if cuts else 1.0
    result = jax.random.normal(stream_key, extent, jnp.float32) * scale * factor_of
    return jnp.minimum(jnp.maximum(result, -most), most).astype(held_as)


def setup_inputs(seed: int = 0) -> dict:
    key_list = jax.random.split(jax.random.key(seed), 9)
    d_field = normal_values(key_list[0], (3, NZ, NX, NY), 1.0, 6.0, ((1, 8), (2, 4)), jnp.float32)
    e_field = normal_values(key_list[1], (3, NZ, NX, NY), 1.0, 6.0, ((1, 8), (2, 4)), jnp.float32)
    h_field = normal_values(key_list[2], (3, NZ, NX, NY), 1.0, 6.0, ((1, 8), (2, 4)), jnp.float32)
    permittivity = jnp.clip(jnp.exp(math.log(4.0) - 1.3862944 * jax.random.uniform(key_list[3], (NZ, NX, NY), jnp.float32) ** block_levels(key_list[3], (NZ, NX, NY), ((0, 8), (1, 4)), -0.2, 0.2)), 1.0, 4.0)
    kerr_coeff = jnp.clip(0.05 + 0.25 * jax.random.uniform(key_list[4], (NZ, NX, NY), jnp.float32) ** block_levels(key_list[4], (NZ, NX, NY), ((0, 8), (1, 4)), -0.2, 0.2), 0.05, 0.3)
    classes = plant(jax.random.randint(key_list[5], (ADVANCE, NX, NY), 0, CLASSES), jax.random.fold_in(key_list[5], 1), 0, CLASSES - 1).astype(jnp.int32)
    eps_table = jnp.clip(jnp.exp(jax.random.uniform(key_list[6], (CLASSES,), jnp.float32, math.log(1.0), math.log(6.0))), 1.0, 6.0)
    chi_table = jnp.clip(jax.random.uniform(key_list[7], (CLASSES,), jnp.float32, 0.02, 0.4), 0.02, 0.4)
    return {"d_field": d_field, "e_field": e_field, "h_field": h_field, "permittivity": permittivity, "kerr_coeff": kerr_coeff, "classes": classes, "eps_table": eps_table, "chi_table": chi_table}


courant = 0.5


def ahead(values, along):
    size = values.shape[along]
    tail = lax.slice_in_dim(values, 1, size, axis=along)
    zeros = jnp.zeros_like(lax.slice_in_dim(values, 0, 1, axis=along))
    return jnp.concatenate([tail, zeros], axis=along)


def behind(values, along):
    size = values.shape[along]
    head = lax.slice_in_dim(values, 0, size - 1, axis=along)
    zeros = jnp.zeros_like(lax.slice_in_dim(values, 0, 1, axis=along))
    return jnp.concatenate([zeros, head], axis=along)


def curl_ahead(field):
    curl_x = (ahead(field[2], 2) - field[2]) - (ahead(field[1], 0) - field[1])
    curl_y = (ahead(field[0], 0) - field[0]) - (ahead(field[2], 1) - field[2])
    curl_z = (ahead(field[1], 1) - field[1]) - (ahead(field[0], 2) - field[0])
    return jnp.stack([curl_x, curl_y, curl_z])


def curl_behind(field):
    curl_x = (field[2] - behind(field[2], 2)) - (field[1] - behind(field[1], 0))
    curl_y = (field[0] - behind(field[0], 0)) - (field[2] - behind(field[2], 1))
    curl_z = (field[1] - behind(field[1], 1)) - (field[0] - behind(field[0], 2))
    return jnp.stack([curl_x, curl_y, curl_z])


def lookup(classes, table):
    labels = jnp.arange(table.shape[0], dtype=jnp.int32).reshape(-1, 1, 1, 1)
    picked = jnp.where(classes[None] == labels, table.reshape(-1, 1, 1, 1), jnp.float32(0.0))
    return jnp.sum(picked, axis=0)


def reference(d_field, e_field, h_field, permittivity, kerr_coeff, classes, eps_table, chi_table):
    displace, electric, magnetic = d_field, e_field, h_field
    for sweep in range(STEPS):
        magnetic = magnetic - courant * curl_ahead(electric)
        displace = displace + courant * curl_behind(magnetic)
        for inner in range(KERR):
            energy = electric[0] * electric[0] + electric[1] * electric[1] + electric[2] * electric[2]
            electric = displace / (permittivity + kerr_coeff * energy)[None]
    zeros = jnp.zeros((3, ADVANCE) + d_field.shape[2:], jnp.float32)
    d_out = jnp.concatenate([displace[:, ADVANCE:], zeros], axis=1)
    e_out = jnp.concatenate([electric[:, ADVANCE:], zeros], axis=1)
    h_out = jnp.concatenate([magnetic[:, ADVANCE:], zeros], axis=1)
    eps_out = jnp.concatenate([permittivity[ADVANCE:], lookup(classes, eps_table)], axis=0)
    chi_out = jnp.concatenate([kerr_coeff[ADVANCE:], lookup(classes, chi_table)], axis=0)
    return d_out, e_out, h_out, eps_out, chi_out
```

```python
import functools

import jax
import jax.numpy as jnp
from jax import lax
from jax.experimental import pallas as pl
from jax.experimental.pallas import tpu as pltpu
from jax.sharding import PartitionSpec as P

STEPS = 4
KERR = 3
ADVANCE = 2
COURANT = 0.5
LOW = STEPS - ADVANCE
HALO = STEPS
MESH = pl.DeviceIdType.MESH


def kernel(
    gz_name, gx_name, gz_count, gx_count,
    d_in, e_in, h_in, eps_in, chi_in, cls_ref, eps_tab, chi_tab,
    d_out, e_out, h_out, eps_out, chi_out,
    F, EX, SE, SU, SL, RU, RL, load_sem, send_sem, recv_sem,
):
    planes, rows, lanes = d_in.shape[1], d_in.shape[2], d_in.shape[3]
    wide = rows + 2 * HALO
    gz = lax.axis_index(gz_name)
    gx = lax.axis_index(gx_name)
    has_dn, has_up = gz > 0, gz < gz_count - 1
    has_lf, has_rt = gx > 0, gx < gx_count - 1
    own = pl.ds(0, rows)
    every = pl.ds(LOW, planes)

    loads = [
        pltpu.make_async_copy(src, F.at[at, every, own], load_sem.at[i])
        for i, (src, at) in enumerate(
            [
                (e_in, pl.ds(0, 3)),
                (h_in, pl.ds(3, 3)),
                (d_in, pl.ds(6, 3)),
                (eps_in, 9),
                (chi_in, 10),
            ]
        )
    ]
    for c in loads:
        c.start()

    barrier = pltpu.get_barrier_semaphore()
    around = []
    for dz in (-1, 0, 1):
        for dx in (-1, 0, 1):
            if dz == 0 and dx == 0:
                continue
            cond = None
            for d, lo, hi in ((dz, has_dn, has_up), (dx, has_lf, has_rt)):
                if d:
                    c = lo if d < 0 else hi
                    cond = c if cond is None else jnp.logical_and(cond, c)
            around.append(((dz, dx), cond))
    conds = dict(around)
    total = jnp.int32(0)
    for (dz, dx), cond in around:
        @pl.when(cond)
        def _(dz=dz, dx=dx):
            pl.semaphore_signal(barrier, inc=1, device_id=(gz + dz, gx + dx), device_id_type=MESH)
        total = total + jnp.where(cond, 1, 0).astype(jnp.int32)
    pl.semaphore_wait(barrier, total)

    n_copy = [0]

    def remote(src, dst, dz, dx):
        i = n_copy[0]
        n_copy[0] += 1
        copy = pltpu.make_async_remote_copy(
            src_ref=src, dst_ref=dst, send_sem=send_sem.at[i], recv_sem=recv_sem.at[i],
            device_id=(gz + dz, gx + dx), device_id_type=MESH,
        )
        return copy, conds[(dz, dx)], conds[(-dz, -dx)]

    def start(group):
        for copy, to, _ in group:
            pl.when(to)(copy.start)

    def arrive(group):
        for copy, _, frm in group:
            pl.when(frm)(copy.wait_recv)

    def sent(group):
        for copy, to, _ in group:
            pl.when(to)(copy.wait_send)

    top = LOW + planes
    last = pl.ds(planes - LOW, LOW)
    up_main = [
        remote(e_in.at[:, last], F.at[pl.ds(0, 3), pl.ds(0, LOW), own], 1, 0),
        remote(h_in.at[:, last], F.at[pl.ds(3, 3), pl.ds(0, LOW), own], 1, 0),
        remote(d_in.at[:, planes - 1], F.at[pl.ds(6, 3), LOW - 1, own], 1, 0),
        remote(eps_in.at[planes - 1], F.at[9, LOW - 1, own], 1, 0),
        remote(chi_in.at[planes - 1], F.at[10, LOW - 1, own], 1, 0),
    ]
    first = pl.ds(0, ADVANCE)
    above = pl.ds(top, ADVANCE)
    dn_main = [
        remote(e_in.at[:, first], F.at[pl.ds(0, 3), above, own], -1, 0),
        remote(h_in.at[:, first], F.at[pl.ds(3, 3), above, own], -1, 0),
        remote(d_in.at[:, first], F.at[pl.ds(6, 3), above, own], -1, 0),
        remote(eps_in.at[first], F.at[9, above, own], -1, 0),
        remote(chi_in.at[first], F.at[10, above, own], -1, 0),
        remote(e_in.at[pl.ds(0, 2), ADVANCE], EX.at[0, :, own], -1, 0),
    ]
    side, up_diag, dn_diag = [], [], []
    for S, R, dx in ((SU, RU, -1), (SL, RL, 1)):
        side.append(remote(S, R.at[:, every], 0, dx))
        up_diag.append(remote(S.at[:, planes - 1], R.at[:, LOW - 1], 1, dx))
        up_diag.append(
            remote(S.at[pl.ds(0, 5), pl.ds(planes - LOW, LOW - 1)], R.at[pl.ds(0, 5), pl.ds(0, LOW - 1)], 1, dx)
        )
        dn_diag.append(remote(S.at[:, first], R.at[:, above], -1, dx))
        dn_diag.append(remote(S.at[pl.ds(0, 2), ADVANCE], R.at[pl.ds(0, 2), top + ADVANCE], -1, dx))
    e_down = [remote(SE.at[s], EX.at[s + 1], -1, 0) for s in range(STEPS - 1)]

    start(up_main)
    for c in loads:
        c.wait()

    def stage(p, carry):
        SU[:, p] = F[:, p + LOW, 0:HALO, :]
        SL[:, p] = F[:, p + LOW, rows - HALO : rows, :]
        return carry

    lax.fori_loop(0, planes, stage, 0)
    start(side)
    start(up_diag)
    start(dn_main)
    start(dn_diag)

    is_top = jnp.logical_not(has_up)

    @pl.when(is_top)
    def _():
        zero = jnp.zeros((wide, lanes), jnp.float32)
        for c in range(2):
            for s in range(STEPS):
                EX[s, c] = zero
        for q in range(ADVANCE):
            cls = cls_ref[q]
            for at, tab in ((9, eps_tab), (10, chi_tab)):
                val = jnp.zeros(cls.shape, jnp.float32)
                for k in range(tab.shape[0]):
                    val = jnp.where(cls == k, tab[k], val)
                F[at, top + q, 0:rows, :] = val
            for c in range(9):
                F[c, top + q, 0:rows, :] = jnp.zeros((rows, lanes), jnp.float32)

    def join(q, count):
        F[0:count, q, rows : rows + HALO, :] = jnp.where(has_rt, RU[0:count, q], 0.0)
        F[0:count, q, rows + HALO : wide, :] = jnp.where(has_lf, RL[0:count, q], 0.0)

    row = lax.broadcasted_iota(jnp.int32, (wide, lanes), 0)
    lane = lax.broadcasted_iota(jnp.int32, (wide, lanes), 1)
    h_off = jnp.logical_and(row >= rows + HALO, jnp.logical_not(has_lf))
    e_off = jnp.logical_and(jnp.logical_and(row >= rows, row < rows + HALO), jnp.logical_not(has_rt))
    lane_end = lane == lanes - 1
    lane_start = lane == 0

    def y_next(v):
        return jnp.where(lane_end, 0.0, pltpu.roll(v, lanes - 1, 1))

    def y_prev(v):
        return jnp.where(lane_start, 0.0, pltpu.roll(v, 1, 1))

    def x_next(v):
        return pltpu.roll(v, wide - 1, 0)

    def x_prev(v):
        return pltpu.roll(v, 1, 0)

    def h_update(q, e_above):
        ex, ey, ez = F[0, q], F[1, q], F[2, q]
        ax, ay = e_above
        off = h_off
        below = jnp.logical_and(q < LOW, jnp.logical_not(has_dn))
        off = jnp.logical_or(off, below)
        hx = F[3, q] - COURANT * ((y_next(ez) - ez) - (ay - ey))
        hy = F[4, q] - COURANT * ((ax - ex) - (x_next(ez) - ez))
        hz = F[5, q] - COURANT * ((x_next(ey) - ey) - (y_next(ex) - ex))
        hx = jnp.where(off, 0.0, hx)
        hy = jnp.where(off, 0.0, hy)
        hz = jnp.where(off, 0.0, hz)
        F[3, q] = hx
        F[4, q] = hy
        F[5, q] = hz
        return (ex, ey, ez), (hx, hy, hz)

    def plane_update(q, e_above, outside):
        (ex, ey, ez), (hx, hy, hz) = h_update(q, e_above)
        bx, by = F[3, q - 1], F[4, q - 1]
        dx = F[6, q] + COURANT * ((hz - y_prev(hz)) - (hy - by))
        dy = F[7, q] + COURANT * ((hx - bx) - (hz - x_prev(hz)))
        dz = F[8, q] + COURANT * ((hy - x_prev(hy)) - (hx - y_prev(hx)))
        F[6, q] = dx
        F[7, q] = dy
        F[8, q] = dz
        eps, chi = F[9, q], F[10, q]
        for _ in range(KERR):
            inv = 1.0 / (eps + chi * (ex * ex + ey * ey + ez * ez))
            ex, ey, ez = dx * inv, dy * inv, dz * inv
        off = jnp.logical_or(e_off, outside)
        F[0, q] = jnp.where(off, 0.0, ex)
        F[1, q] = jnp.where(off, 0.0, ey)
        F[2, q] = jnp.where(off, 0.0, ez)

    def from_above(q):
        return F[0, q + 1], F[1, q + 1]

    def sweep(q, carry):
        plane_update(q, from_above(q), jnp.logical_and(q >= top, is_top))
        return carry

    arrive(side)

    def join_own(q, carry):
        join(q, 11)
        return carry

    lax.fori_loop(LOW, top, join_own, 0)
    arrive(up_main)
    arrive(up_diag)
    for q in range(LOW - 1):
        join(q, 5)
    join(LOW - 1, 11)

    for s in range(1, STEPS + 1):
        h_update(s - 1, from_above(s - 1))
        lax.fori_loop(s, top - s, sweep, 0)
        if s < STEPS:
            SE[s - 1] = F[0:2, LOW + ADVANCE]
            start(e_down[s - 1 : s])

    arrive(dn_main)
    arrive(dn_diag)
    for q in range(ADVANCE):
        join(top + q, 11)
    EX[0, :, rows : rows + HALO, :] = jnp.where(has_rt, RU[0:2, top + ADVANCE], 0.0)
    EX[0, :, rows + HALO : wide, :] = jnp.where(has_lf, RL[0:2, top + ADVANCE], 0.0)

    @pl.when(is_top)
    def _():
        for c in range(9):
            for q in range(ADVANCE):
                F[c, top + q] = jnp.zeros((wide, lanes), jnp.float32)
        EX[0] = jnp.zeros((2, wide, lanes), jnp.float32)

    for s in range(1, STEPS + 1):
        lax.fori_loop(top - s, top + ADVANCE - 1, sweep, 0)
        if s > 1:
            arrive(e_down[s - 2 : s - 1])
        q = top + ADVANCE - 1
        plane_update(q, (EX[s - 1, 0], EX[s - 1, 1]), is_top)

    @pl.when(is_top)
    def _():
        for c in range(3, 9):
            for q in range(ADVANCE):
                F[c, top + q] = jnp.zeros((wide, lanes), jnp.float32)

    moved = pl.ds(LOW + ADVANCE, planes)
    stores = [
        pltpu.make_async_copy(F.at[at, moved, own], dst, load_sem.at[i])
        for i, (dst, at) in enumerate(
            [
                (e_out, pl.ds(0, 3)),
                (h_out, pl.ds(3, 3)),
                (d_out, pl.ds(6, 3)),
                (eps_out, 9),
                (chi_out, 10),
            ]
        )
    ]
    for c in stores:
        c.start()
    for group in (up_main, side, up_diag, dn_main, dn_diag, e_down):
        sent(group)
    for c in stores:
        c.wait()


N_COPIES = 5 + 6 + 10 + STEPS - 1


def on_device(mesh, d_field, e_field, h_field, permittivity, kerr_coeff, classes, eps_table, chi_table):
    gz_name, gx_name = mesh.axis_names
    _, planes, rows, lanes = d_field.shape
    wide = rows + 2 * HALO
    depth = LOW + planes + ADVANCE
    f32 = jnp.float32
    hbm = pl.BlockSpec(memory_space=pl.ANY)
    smem = pl.BlockSpec(memory_space=pltpu.SMEM)
    vmem = pl.BlockSpec(memory_space=pltpu.VMEM)
    return pl.pallas_call(
        functools.partial(kernel, gz_name, gx_name, mesh.shape[gz_name], mesh.shape[gx_name]),
        out_shape=[jax.ShapeDtypeStruct(a.shape, f32) for a in (d_field, e_field, h_field, permittivity, kerr_coeff)],
        in_specs=[hbm] * 5 + [vmem, smem, smem],
        out_specs=[hbm] * 5,
        scratch_shapes=[
            pltpu.VMEM((11, depth, wide, lanes), f32),
            pltpu.VMEM((STEPS, 2, wide, lanes), f32),
            pltpu.VMEM((STEPS - 1, 2, wide, lanes), f32),
            pltpu.VMEM((11, planes, HALO, lanes), f32),
            pltpu.VMEM((11, planes, HALO, lanes), f32),
            pltpu.VMEM((11, depth + 1, HALO, lanes), f32),
            pltpu.VMEM((11, depth + 1, HALO, lanes), f32),
            pltpu.SemaphoreType.DMA((5,)),
            pltpu.SemaphoreType.DMA((N_COPIES,)),
            pltpu.SemaphoreType.DMA((N_COPIES,)),
        ],
        compiler_params=pltpu.CompilerParams(
            collective_id=0, has_side_effects=True, vmem_limit_bytes=32 * 1024 * 1024
        ),
        name="window",
    )(d_field, e_field, h_field, permittivity, kerr_coeff, classes, eps_table, chi_table)


def solution(mesh):
    field = P(None, "gz", "gx", None)
    cell = P("gz", "gx", None)
    return jax.shard_map(
        functools.partial(on_device, mesh),
        mesh=mesh,
        in_specs=(field, field, field, cell, cell, P(None, "gx", None), P(), P()),
        out_specs=(field, field, field, cell, cell),
        check_vma=False,
    )
```

```python
import functools

import jax
import jax.numpy as jnp
from jax import lax
from jax.experimental import pallas as pl
from jax.experimental.pallas import tpu as pltpu
from jax.sharding import PartitionSpec as P

STEPS = 4
KERR = 3
ADVANCE = 2
COURANT = 0.5
LOW = STEPS - ADVANCE
HALO = STEPS
MESH = pl.DeviceIdType.MESH


def kernel(
    gz_name, gx_name, gz_count, gx_count,
    d_in, e_in, h_in, eps_in, chi_in, cls_in, eps_tab_in, chi_tab_in,
    d_out, e_out, h_out, eps_out, chi_out,
    F, EX, SE, HX, SU, SL, RU, RL, cls_ref, eps_tab, chi_tab, load_sem, send_sem, recv_sem,
):
    planes, rows, lanes = d_in.shape[1], d_in.shape[2], d_in.shape[3]
    wide = rows + 2 * HALO
    gz = lax.axis_index(gz_name)
    gx = lax.axis_index(gx_name)
    has_dn, has_up = gz > 0, gz < gz_count - 1
    has_lf, has_rt = gx > 0, gx < gx_count - 1
    own = pl.ds(0, rows)
    every = pl.ds(LOW, planes)

    loads = [
        pltpu.make_async_copy(src, F.at[at, every, own], load_sem.at[i])
        for i, (src, at) in enumerate(
            [
                (e_in, pl.ds(0, 3)),
                (h_in, pl.ds(3, 3)),
                (d_in, pl.ds(6, 3)),
                (eps_in, 9),
                (chi_in, 10),
            ]
        )
    ]
    extra = [
        pltpu.make_async_copy(src, dst, load_sem.at[5 + i])
        for i, (src, dst) in enumerate([(cls_in, cls_ref), (eps_tab_in, eps_tab), (chi_tab_in, chi_tab)])
    ]
    for c in loads + extra:
        c.start()

    barrier = pltpu.get_barrier_semaphore()
    around = []
    for dz in (-1, 0, 1):
        for dx in (-1, 0, 1):
            if dz == 0 and dx == 0:
                continue
            cond = None
            for d, lo, hi in ((dz, has_dn, has_up), (dx, has_lf, has_rt)):
                if d:
                    c = lo if d < 0 else hi
                    cond = c if cond is None else jnp.logical_and(cond, c)
            around.append(((dz, dx), cond))
    conds = dict(around)
    total = jnp.int32(0)
    for (dz, dx), cond in around:
        @pl.when(cond)
        def _(dz=dz, dx=dx):
            pl.semaphore_signal(barrier, inc=1, device_id=(gz + dz, gx + dx), device_id_type=MESH)
        total = total + jnp.where(cond, 1, 0).astype(jnp.int32)
    pl.semaphore_wait(barrier, total)

    n_copy = [0]

    def remote(src, dst, dz, dx):
        i = n_copy[0]
        n_copy[0] += 1
        copy = pltpu.make_async_remote_copy(
            src_ref=src, dst_ref=dst, send_sem=send_sem.at[i], recv_sem=recv_sem.at[i],
            device_id=(gz + dz, gx + dx), device_id_type=MESH,
        )
        return copy, conds[(dz, dx)], conds[(-dz, -dx)]

    def start(group):
        for copy, to, _ in group:
            pl.when(to)(copy.start)

    def arrive(group):
        for copy, _, frm in group:
            pl.when(frm)(copy.wait_recv)

    def sent(group):
        for copy, to, _ in group:
            pl.when(to)(copy.wait_send)

    top = LOW + planes
    up_main = [
        remote(e_in.at[:, planes - 1], F.at[pl.ds(0, 3), LOW - 1, own], 1, 0),
        remote(h_in.at[pl.ds(0, 2), planes - 1], F.at[pl.ds(3, 2), LOW - 1, own], 1, 0),
    ]
    first = pl.ds(0, ADVANCE)
    above = pl.ds(top, ADVANCE)
    dn_main = [
        remote(e_in.at[:, first], F.at[pl.ds(0, 3), above, own], -1, 0),
        remote(h_in.at[:, first], F.at[pl.ds(3, 3), above, own], -1, 0),
        remote(d_in.at[:, first], F.at[pl.ds(6, 3), above, own], -1, 0),
        remote(eps_in.at[first], F.at[9, above, own], -1, 0),
        remote(chi_in.at[first], F.at[10, above, own], -1, 0),
        remote(e_in.at[pl.ds(0, 2), ADVANCE], EX.at[0, :, own], -1, 0),
    ]
    side, up_diag, dn_diag = [], [], []
    for S, R, dx in ((SU, RU, -1), (SL, RL, 1)):
        side.append(remote(S, R.at[:, every], 0, dx))
        up_diag.append(remote(S.at[pl.ds(0, 5), planes - 1], R.at[pl.ds(0, 5), LOW - 1], 1, dx))
        dn_diag.append(remote(S.at[:, first], R.at[:, above], -1, dx))
        dn_diag.append(remote(S.at[pl.ds(0, 2), ADVANCE], R.at[pl.ds(0, 2), top + ADVANCE], -1, dx))
    e_down = [remote(SE.at[s], EX.at[s + 1], -1, 0) for s in range(STEPS - 1)]

    h_up = [remote(F.at[pl.ds(3, 2), top + ADVANCE - 1], HX, 1, 0)]

    start(up_main)
    for c in loads:
        c.wait()

    def stage(p, carry):
        SU[:, p] = F[:, p + LOW, 0:HALO, :]
        SL[:, p] = F[:, p + LOW, rows - HALO : rows, :]
        return carry

    lax.fori_loop(0, planes, stage, 0)
    start(side)
    start(up_diag)
    start(dn_main)
    start(dn_diag)

    is_top = jnp.logical_not(has_up)
    for c in extra:
        c.wait()

    @pl.when(is_top)
    def _():
        zero = jnp.zeros((wide, lanes), jnp.float32)
        for c in range(2):
            for s in range(STEPS):
                EX[s, c] = zero
        for q in range(ADVANCE):
            cls = cls_ref[q]
            for at, tab in ((9, eps_tab), (10, chi_tab)):
                val = jnp.zeros(cls.shape, jnp.float32)
                for k in range(tab.shape[0]):
                    val = jnp.where(cls == k, tab[k], val)
                F[at, top + q, 0:rows, :] = val
            for c in range(9):
                F[c, top + q, 0:rows, :] = jnp.zeros((rows, lanes), jnp.float32)

    def join(q, count):
        F[0:count, q, rows : rows + HALO, :] = jnp.where(has_rt, RU[0:count, q], 0.0)
        F[0:count, q, rows + HALO : wide, :] = jnp.where(has_lf, RL[0:count, q], 0.0)

    row = lax.broadcasted_iota(jnp.int32, (wide, lanes), 0)
    lane = lax.broadcasted_iota(jnp.int32, (wide, lanes), 1)
    h_off = jnp.logical_and(row >= rows + HALO, jnp.logical_not(has_lf))
    e_off = jnp.logical_and(jnp.logical_and(row >= rows, row < rows + HALO), jnp.logical_not(has_rt))
    lane_end = lane == lanes - 1
    lane_start = lane == 0

    def y_next(v):
        return jnp.where(lane_end, 0.0, pltpu.roll(v, lanes - 1, 1))

    def y_prev(v):
        return jnp.where(lane_start, 0.0, pltpu.roll(v, 1, 1))

    def x_next(v):
        return pltpu.roll(v, wide - 1, 0)

    def x_prev(v):
        return pltpu.roll(v, 1, 0)

    def h_update(q, e_above):
        ex, ey, ez = F[0, q], F[1, q], F[2, q]
        ax, ay = e_above
        off = h_off
        below = jnp.logical_and(q < LOW, jnp.logical_not(has_dn))
        off = jnp.logical_or(off, below)
        hx = F[3, q] - COURANT * ((y_next(ez) - ez) - (ay - ey))
        hy = F[4, q] - COURANT * ((ax - ex) - (x_next(ez) - ez))
        hz = F[5, q] - COURANT * ((x_next(ey) - ey) - (y_next(ex) - ex))
        hx = jnp.where(off, 0.0, hx)
        hy = jnp.where(off, 0.0, hy)
        hz = jnp.where(off, 0.0, hz)
        F[3, q] = hx
        F[4, q] = hy
        F[5, q] = hz
        return (ex, ey, ez), (hx, hy, hz)

    def de_update(q, e_old, h_new, below, outside):
        (ex, ey, ez), (hx, hy, hz), (bx, by) = e_old, h_new, below
        dx = F[6, q] + COURANT * ((hz - y_prev(hz)) - (hy - by))
        dy = F[7, q] + COURANT * ((hx - bx) - (hz - x_prev(hz)))
        dz = F[8, q] + COURANT * ((hy - x_prev(hy)) - (hx - y_prev(hx)))
        F[6, q] = dx
        F[7, q] = dy
        F[8, q] = dz
        eps, chi = F[9, q], F[10, q]
        for _ in range(KERR):
            inv = 1.0 / (eps + chi * (ex * ex + ey * ey + ez * ez))
            ex, ey, ez = dx * inv, dy * inv, dz * inv
        off = jnp.logical_or(e_off, outside)
        F[0, q] = jnp.where(off, 0.0, ex)
        F[1, q] = jnp.where(off, 0.0, ey)
        F[2, q] = jnp.where(off, 0.0, ez)

    def plane_update(q, e_above, outside):
        e_old, h_new = h_update(q, e_above)
        de_update(q, e_old, h_new, (F[3, q - 1], F[4, q - 1]), outside)

    def from_above(q):
        return F[0, q + 1], F[1, q + 1]

    def sweep(q, carry):
        plane_update(q, from_above(q), jnp.logical_and(q >= top, is_top))
        return carry

    arrive(side)

    def join_own(q, carry):
        join(q, 11)
        return carry

    lax.fori_loop(LOW, top, join_own, 0)
    arrive(up_main)
    arrive(up_diag)
    join(LOW - 1, 5)

    for s in range(1, STEPS + 1):
        low = jnp.where(has_dn, LOW - 1 + s, LOW).astype(jnp.int32)
        h_update(low - 1, from_above(low - 1))
        lax.fori_loop(low, top - s, sweep, 0)
        if s < STEPS:
            SE[s - 1] = F[0:2, LOW + ADVANCE]
            start(e_down[s - 1 : s])

    arrive(dn_main)
    arrive(dn_diag)
    for q in range(ADVANCE):
        join(top + q, 11)
    EX[0, :, rows : rows + HALO, :] = jnp.where(has_rt, RU[0:2, top + ADVANCE], 0.0)
    EX[0, :, rows + HALO : wide, :] = jnp.where(has_lf, RL[0:2, top + ADVANCE], 0.0)

    @pl.when(is_top)
    def _():
        for c in range(9):
            for q in range(ADVANCE):
                F[c, top + q] = jnp.zeros((wide, lanes), jnp.float32)
        EX[0] = jnp.zeros((2, wide, lanes), jnp.float32)

    edge = top + ADVANCE - 1
    for s in range(1, STEPS):
        lax.fori_loop(top - s, edge, sweep, 0)
        if s > 1:
            arrive(e_down[s - 2 : s - 1])
        plane_update(edge, (EX[s - 1, 0], EX[s - 1, 1]), is_top)
    arrive(e_down[STEPS - 2 :])
    h_update(edge, (EX[STEPS - 1, 0], EX[STEPS - 1, 1]))
    start(h_up)
    lax.fori_loop(top - STEPS, edge, sweep, 0)

    def held(c, q):
        return F[c, q], F[c + 1, q], F[c + 2, q]

    de_update(edge, held(0, edge), held(3, edge), (F[3, edge - 1], F[4, edge - 1]), is_top)

    @pl.when(is_top)
    def _():
        for c in range(3, 9):
            for q in range(ADVANCE):
                F[c, top + q] = jnp.zeros((wide, lanes), jnp.float32)

    begin = LOW + ADVANCE
    moved = pl.ds(begin, planes)
    rest = pl.ds(begin + 1, planes - 1)
    later = pl.ds(1, planes - 1)
    stores = [
        pltpu.make_async_copy(src, dst, load_sem.at[i])
        for i, (src, dst) in enumerate(
            [
                (F.at[pl.ds(3, 3), moved, own], h_out),
                (F.at[9, moved, own], eps_out),
                (F.at[10, moved, own], chi_out),
                (F.at[pl.ds(0, 3), rest, own], e_out.at[:, later]),
                (F.at[pl.ds(6, 3), rest, own], d_out.at[:, later]),
                (F.at[pl.ds(0, 3), begin, own], e_out.at[:, 0]),
                (F.at[pl.ds(6, 3), begin, own], d_out.at[:, 0]),
            ]
        )
    ]
    for c in stores[:5]:
        c.start()
    arrive(h_up)

    @pl.when(has_dn)
    def _():
        de_update(begin, held(0, begin), held(3, begin), (HX[0], HX[1]), False)

    for c in stores[5:]:
        c.start()
    for group in (up_main, side, up_diag, dn_main, dn_diag, e_down, h_up):
        sent(group)
    for c in stores:
        c.wait()


def copy_kernel(*refs):
    count = len(refs) // 2
    sem = refs[-1]
    copies = [pltpu.make_async_copy(refs[i], refs[count + i], sem.at[i]) for i in range(count)]
    for c in copies:
        c.start()
    for c in copies:
        c.wait()


N_COPIES = 2 + 6 + 8 + STEPS - 1 + 1


def on_device(mesh, d_field, e_field, h_field, permittivity, kerr_coeff, classes, eps_table, chi_table):
    gz_name, gx_name = mesh.axis_names
    _, planes, rows, lanes = d_field.shape
    wide = rows + 2 * HALO
    depth = LOW + planes + ADVANCE
    f32 = jnp.float32
    hbm = pl.BlockSpec(memory_space=pltpu.HBM)
    results = pl.pallas_call(
        functools.partial(kernel, gz_name, gx_name, mesh.shape[gz_name], mesh.shape[gx_name]),
        out_shape=[jax.ShapeDtypeStruct(a.shape, f32) for a in (d_field, e_field, h_field, permittivity, kerr_coeff)],
        in_specs=[hbm] * 8,
        out_specs=[hbm] * 5,
        scratch_shapes=[
            pltpu.VMEM((11, depth, wide, lanes), f32),
            pltpu.VMEM((STEPS, 2, wide, lanes), f32),
            pltpu.VMEM((STEPS - 1, 2, wide, lanes), f32),
            pltpu.VMEM((2, wide, lanes), f32),
            pltpu.VMEM((11, planes, HALO, lanes), f32),
            pltpu.VMEM((11, planes, HALO, lanes), f32),
            pltpu.VMEM((11, depth + 1, HALO, lanes), f32),
            pltpu.VMEM((11, depth + 1, HALO, lanes), f32),
            pltpu.VMEM(classes.shape, jnp.int32),
            pltpu.SMEM(eps_table.shape, f32),
            pltpu.SMEM(chi_table.shape, f32),
            pltpu.SemaphoreType.DMA((8,)),
            pltpu.SemaphoreType.DMA((N_COPIES,)),
            pltpu.SemaphoreType.DMA((N_COPIES,)),
        ],
        compiler_params=pltpu.CompilerParams(
            collective_id=0, has_side_effects=True, vmem_limit_bytes=60 * 1024 * 1024
        ),
        name="window",
    )(d_field, e_field, h_field, permittivity, kerr_coeff, classes, eps_table, chi_table)
    return pl.pallas_call(
        copy_kernel,
        out_shape=[jax.ShapeDtypeStruct(r.shape, f32) for r in results],
        in_specs=[hbm] * 5,
        out_specs=[hbm] * 5,
        scratch_shapes=[pltpu.SemaphoreType.DMA((5,))],
        compiler_params=pltpu.CompilerParams(vmem_limit_bytes=60 * 1024 * 1024),
        name="place",
    )(*results)


def solution(mesh):
    field = P(None, "gz", "gx", None)
    cell = P("gz", "gx", None)
    return jax.shard_map(
        functools.partial(on_device, mesh),
        mesh=mesh,
        in_specs=(field, field, field, cell, cell, P(None, "gx", None), P(), P()),
        out_specs=(field, field, field, cell, cell),
        check_vma=False,
    )
```
